256 devices in a mesh: eig: 16 (over x, z_hi, core), store: 16 (over z_lo, y).
Axes of the slice: x: 4, y: 4, z: 8 (z_hi: 2, z_lo: 4; z = z_hi * 4 + z_lo), core: 2. Of those that a mesh axis runs over, the one named last changes fastest.
Arguments:
- acts: bfloat16 [2048, 8192], P('store'), may hold values from -6 to 6
- basis: bfloat16 [8192, 8192], P('store', 'eig'), may hold values from -0.0625 to 0.0625
- eigvals: float32 [64, 8192], P(None, 'eig'), may hold values from 0.5 to 8
- projection: bfloat16 [8192, 64], P('eig'), may hold values from -0.0625 to 0.0625
- out_factor: float32 [2048, 64], P('store', 'eig'), may hold values from -6 to 6
- store: bfloat16 [32768, 4096], P('store', 'eig'), may hold values from -0.09375 to 0.09375
Outputs:
- scores: float32 [2048, 32768], P(None, ('store', 'eig'))
The draws below stay inside these ranges and needn't reach their ends.
All inputs are finite; a program needn't handle non-finite values.
Results may differ from the reference program's by a relative error of at most 0.0041.
Values may be sent and summed in bfloat16 or wider, within the bound.
A program may use at most 64 MiB of HBM per device.

```python
import math
import jax
import jax.numpy as jnp
from jax import lax

D = 8192
K_OUT = 64
K_IN = 64
NQ = 2048
STORE = 32768
PROJ = 4096


def block_scale(own_key, extent, shards, smallest, largest):
    factor_of, own = 1.0, jax.random.fold_in(own_key, 6)
    for axis_at, shards_of in shards:
        heights = jnp.exp(jax.random.uniform(jax.random.fold_in(own, axis_at), (shards_of,), jnp.float32, smallest / len(shards), largest / len(shards)))
        factor_of = factor_of * jnp.repeat(heights, extent[axis_at] // shards_of).reshape([-1 if axis == axis_at else 1 for axis in range(len(extent))])
    return factor_of


def scatter_about(own_key, dims, spread, bound, pieces=(), held_as=jnp.bfloat16):
    drawn = jax.random.normal(own_key, dims, jnp.float32) * spread
    if len(pieces) > 0:
        drawn = block_scale(own_key, dims, pieces, -0.22, 0.18) * drawn
    return jnp.clip(drawn, min=-bound, max=bound).astype(held_as)


def setup_inputs(seed: int = 0) -> dict:
    seeds = jax.random.split(jax.random.key(seed), 7)
    acts = scatter_about(seeds[0], (NQ, D), 1.0, 6.0, ((0, 16),))
    basis = scatter_about(seeds[1], (D, D), D ** -0.5, 0.0625, ((0, 16), (1, 16)))
    eigvals = jnp.clip(jnp.exp(math.log(8.0) - 2.7725887 * jax.random.uniform(seeds[2], (K_OUT, D), jnp.float32) ** block_scale(seeds[2], (K_OUT, D), ((1, 16),), -0.2, 0.2)), 0.5, 8.0)
    projection = scatter_about(seeds[3], (D, K_IN), D ** -0.5, 0.0625, ((0, 16),))
    out_factor = scatter_about(seeds[4], (NQ, K_OUT), 1.0, 6.0, ((0, 16), (1, 16)), jnp.float32)
    store = scatter_about(seeds[5], (STORE, PROJ), PROJ ** -0.5, 0.09375, ((0, 16), (1, 16)))
    return dict(acts=acts, basis=basis, eigvals=eigvals, projection=projection, out_factor=out_factor, store=store)


damping = 0.1


def reference(acts, basis, eigvals, projection, out_factor, store):
    rotated = jnp.dot(acts, basis, preferred_element_type=jnp.float32)
    inverse = 1.0 / (eigvals + damping)

    def project_component(row_inverse):
        scaled = (rotated * row_inverse[None, :]).astype(jnp.bfloat16)
        return jnp.dot(scaled, projection, preferred_element_type=jnp.float32)

    summed = lax.map(project_component, inverse)
    summed = jnp.transpose(summed, (1, 0, 2))
    features = (summed * out_factor[:, :, None]).reshape(NQ, K_OUT * K_IN).astype(jnp.bfloat16)
    return jnp.dot(features, store.T, preferred_element_type=jnp.float32)
```

```python
import jax
import jax.numpy as jnp
from jax import lax
from jax.experimental import pallas as pl
from jax.experimental.pallas import tpu as pltpu
from jax.sharding import PartitionSpec as P

damping = 0.1
NT = (((1,), (1,)), ((), ()))


def at(x, zh, c, zl, y):
    return {"eig": x * 4 + zh * 2 + c, "store": zl * 4 + y}


def send(src, dst, sems, index, device):
    copy = pltpu.make_async_remote_copy(
        src_ref=src,
        dst_ref=dst,
        send_sem=sems.at[(0, *index)],
        recv_sem=sems.at[(1, *index)],
        device_id=device,
        device_id_type=pl.DeviceIdType.MESH,
    )
    copy.start()
    return copy


def kernel(
    acts, basis, inverse, projection, factor, store, out,
    acts_g, basis_g, part, landed, rotated, inv_g, proj_g, fac_g, store_g,
    summed, summed_in, feats, going, coming,
    own_sem, basis_sem, az_sem, ax_sem, ac_sem, st_sem, iv_sem, pr_sem, of_sem,
    zr_sem, rc_sem, cx_sem, fz_sem, fy_sem, fc_sem, sx_sem,
):
    e, s = lax.axis_index("eig"), lax.axis_index("store")
    x, zh, c = lax.div(e, 4), lax.rem(lax.div(e, 2), 2), lax.rem(e, 2)
    zl, y = lax.div(s, 4), lax.rem(s, 4)
    z = zh * 4 + zl
    piece = x * 2 + c

    def off(value, step, extent):
        return lax.rem(value + step, extent)

    def along_x(d):
        return at(off(x, d, 4), zh, c, zl, y)

    def along_y(d):
        return at(x, zh, c, zl, off(y, d, 4))

    def along_z(d):
        to = off(z, d, 8)
        return at(x, lax.div(to, 4), c, lax.rem(to, 4), y)

    def within_line(d):
        return at(x, zh, c, off(zl, d, 4), y)

    def flipped(m):
        to_h = 1 - zh if m & 2 else zh
        to_c = 1 - c if m & 1 else c
        return at(x, to_h, to_c, zl, y)

    sibling = flipped(1)

    own = [
        pltpu.make_async_copy(basis, basis_g.at[y], own_sem.at[0]),
        pltpu.make_async_copy(acts.at[:, pl.ds(pl.multiple_of(zl * 2048, 2048), 2048)], acts_g.at[zl], own_sem.at[1]),
        pltpu.make_async_copy(inverse.at[c], inv_g.at[0], own_sem.at[2]),
        pltpu.make_async_copy(projection, proj_g.at[0], own_sem.at[3]),
        pltpu.make_async_copy(factor.at[zh], fac_g.at[zh], own_sem.at[4]),
    ]
    for d in range(4):
        own.append(pltpu.make_async_copy(store.at[off(x, d, 4), zh, c], store_g.at[0, d], own_sem.at[5 + d]))
    for copy in own:
        copy.start()

    barrier = pltpu.get_barrier_semaphore()
    partners = [along_x(d) for d in range(1, 4)] + [along_y(d) for d in range(1, 4)]
    partners += [along_z(d) for d in range(1, 8)] + [sibling, flipped(3)]
    for partner in partners:
        pl.semaphore_signal(barrier, inc=1, device_id=partner, device_id_type=pl.DeviceIdType.MESH)
    pl.semaphore_wait(barrier, len(partners))

    rows = pl.ds(pl.multiple_of(piece * 16, 16), 16)
    line = []
    for d in range(1, 4):
        to = off(zl, d, 4)
        line.append(
            send(
                acts.at[rows, pl.ds(pl.multiple_of(to * 2048, 2048), 2048)],
                acts_g.at[zl, rows],
                az_sem, (d - 1,), within_line(d),
            )
        )
    blocks = [send(basis, basis_g.at[y], basis_sem, (d - 1,), along_y(d)) for d in (1, 3, 2)]
    shared, paired = [], []
    for d in range(1, 4):
        line[d - 1].wait_recv()
        slot = acts_g.at[off(zl, 4 - d, 4), rows]
        for dx in (1, 3, 2):
            shared.append((d, dx, send(slot, slot, ax_sem, (d - 1, dx - 1), along_x(dx))))
        paired.append(send(slot, slot, ac_sem, (d - 1, 0), sibling))

    behind = []
    for m in range(1, 4):
        to_h = 1 - zh if m & 2 else zh
        to_c = 1 - c if m & 1 else c
        behind.append(send(inverse.at[to_c], inv_g.at[m], iv_sem, (m - 1,), flipped(m)))
        behind.append(send(projection, proj_g.at[m], pr_sem, (m - 1,), flipped(m)))
    behind.append(send(factor.at[1 - zh], fac_g.at[zh], of_sem, (0,), flipped(2)))
    later = []
    for m in range(1, 4):
        to_h = 1 - zh if m & 2 else zh
        to_c = 1 - c if m & 1 else c
        for d in range(4):
            later.append(send(store.at[off(x, d, 4), to_h, to_c], store_g.at[m, d], st_sem, (m - 1, d), flipped(m)))

    for d, dx, copy in shared:
        copy.wait_recv()
        theirs = pl.ds(pl.multiple_of((off(x, 4 - dx, 4) * 2 + c) * 16, 16), 16)
        slot = acts_g.at[off(zl, 4 - d, 4), theirs]
        paired.append(send(slot, slot, ac_sem, (d - 1, dx), sibling))
    for copy in own[:2]:
        copy.wait()
    for copy in paired:
        copy.wait_recv()
    for copy in blocks:
        copy.wait_recv()

    partial = []
    for d in (2, 1, 3, 0):
        to = off(zl, d, 4)
        value = jnp.dot(acts_g[to], basis_g[...].reshape(2048, 512), preferred_element_type=jnp.float32)
        part[to] = value.reshape(2, 64, 512)
        for h in range(2):
            step = (4 * h + d) % 8
            if step == 0:
                continue
            to_h = 1 - zh if h else zh
            partial.append(
                send(part.at[to, to_h], landed.at[h, d], zr_sem, (h, d), at(x, to_h, c, to, y))
            )
    landed[0, 0] = part[zl, zh]
    for copy in partial:
        copy.wait_recv()
    for h in range(2):
        total = (landed[h, 0] + landed[h, 1]) + (landed[h, 2] + landed[h, 3])
        rotated[0, h] = total
    across = send(rotated.at[0], rotated.at[1], rc_sem, (0,), sibling)

    for copy in own[2:]:
        copy.wait()
    for copy in behind:
        copy.wait_recv()
    across.wait_recv()

    lanes = lax.broadcasted_iota(jnp.int32, (128, 256), 1)
    scattered = []
    for d in (2, 1, 3, 0):
        value = jnp.zeros((512, 256), jnp.float32)
        for m in range(4):
            heights = inv_g[m, off(x, d, 4)]
            scaled = (rotated[m & 1, m >> 1][None, :, :] * heights[:, None, :]).astype(jnp.bfloat16)
            block = proj_g[m]
            value += lax.dot_general(
                scaled.reshape(512, 512), jnp.concatenate([block] * 4, axis=0), NT,
                preferred_element_type=jnp.float32,
            )
        value = value.reshape(4, 128, 256)
        picked = jnp.where(
            lanes < 128,
            jnp.where(lanes < 64, value[0], value[1]),
            jnp.where(lanes < 192, value[2], value[3]),
        )
        summed[d] = picked.reshape(2, 64, 256)
        if d:
            scattered.append(send(summed.at[d], summed_in.at[d - 1], cx_sem, (d - 1,), along_x(d)))
    for copy in scattered:
        copy.wait_recv()
    total = (summed[0] + summed_in[0]) + (summed_in[1] + summed_in[2])
    feats[c, y, z] = (total * fac_g[...]).astype(jnp.bfloat16)

    mine = feats.at[c, y, z]
    ring = [send(mine, mine, fz_sem, (d - 1,), along_z(d)) for d in (1, 7, 2, 6, 3, 5, 4)]
    for copy in ring:
        copy.wait_recv()
    mine = feats.at[c, y]
    plane = {0: send(mine, mine, fc_sem, (0,), sibling)}
    gathered = {d: send(mine, mine, fy_sem, (d - 1,), along_y(d)) for d in (1, 3, 2)}
    for copy in later:
        copy.wait_recv()

    reduced = []
    for d in (0, 1, 3, 2):
        at_y = off(y, 4 - d, 4)
        if d:
            gathered[d].wait_recv()
            theirs = feats.at[c, at_y]
            plane[d] = send(theirs, theirs, fc_sem, (d,), sibling)
        plane[d].wait_recv()

        def tile(j, carry):
            value = jnp.zeros((128, 512), jnp.float32)
            for m in range(4):
                at_c = 1 - c if m & 1 else c
                at_h = 1 - zh if m & 2 else zh
                left = feats[at_c, at_y, pl.ds(j * 2, 2), at_h].reshape(128, 256)
                value += lax.dot_general(
                    left, store_g[m].reshape(512, 256), NT, preferred_element_type=jnp.float32
                )
            for half in range(2):
                rows_of = value[half * 64 : half * 64 + 64]
                at_z = j * 2 + half
                out[lax.rem(at_z, 4), at_y, lax.div(at_z, 4)] = rows_of[:, :128]
                for k in range(1, 4):
                    going[k - 1, d, at_z] = rows_of[:, k * 128 : k * 128 + 128].astype(jnp.bfloat16)
            return carry

        lax.fori_loop(0, 4, tile, 0)
        for k in (2, 1, 3):
            reduced.append(
                send(going.at[k - 1, d], coming.at[k - 1, d], sx_sem, (k - 1, d), along_x(k))
            )
    for d in (0, 1, 3, 2):
        at_y = off(y, 4 - d, 4)
        for copy in reduced[:3]:
            copy.wait_recv()
        waited, reduced = reduced[:3], reduced[3:]

        def add(j, carry):
            at_l, at_h = lax.rem(j, 4), lax.div(j, 4)
            rest = coming[0, d, j].astype(jnp.float32) + coming[1, d, j].astype(jnp.float32)
            out[at_l, at_y, at_h] = out[at_l, at_y, at_h] + (rest + coming[2, d, j].astype(jnp.float32))
            return carry

        lax.fori_loop(0, 8, add, 0)
        for copy in waited:
            copy.wait_send()

    sent = line + blocks + [copy for _, _, copy in shared] + paired + behind + later
    sent += partial + [across] + scattered + ring + list(plane.values()) + list(gathered.values())
    for copy in sent:
        copy.wait_send()


def body(acts, basis, eigvals, projection, out_factor, store):
    bf16, f32 = jnp.bfloat16, jnp.float32
    inverse = 1.0 / (eigvals + damping)
    inverse = inverse.reshape(4, 2, 2, 4, 512).transpose(2, 0, 3, 1, 4).reshape(2, 4, 8, 512)
    factor = jnp.repeat(out_factor, 64, axis=1).reshape(2, 64, 256)
    sems = [(9,)] + [
        (2, *n)
        for n in [(3,), (3,), (3, 3), (3, 4), (3, 4), (3,), (3,), (1,), (2, 4), (1,), (3,), (7,), (3,), (4,), (3, 4)]
    ]
    vmem = pl.BlockSpec(memory_space=pltpu.VMEM)
    hbm = pl.BlockSpec(memory_space=pl.ANY)
    scores = pl.pallas_call(
        kernel,
        out_shape=jax.ShapeDtypeStruct((4, 4, 2, 64, 128), f32),
        in_specs=[hbm, hbm, vmem, vmem, vmem, hbm],
        out_specs=vmem,
        scratch_shapes=[
            pltpu.VMEM((4, 128, 2048), bf16),
            pltpu.VMEM((4, 512, 512), bf16),
            pltpu.VMEM((4, 2, 64, 512), f32),
            pltpu.VMEM((2, 4, 64, 512), f32),
            pltpu.VMEM((2, 2, 64, 512), f32),
            pltpu.VMEM((4, 4, 8, 512), f32),
            pltpu.VMEM((4, 64, 512), bf16),
            pltpu.VMEM((2, 64, 256), f32),
            pltpu.VMEM((4, 4, 128, 256), bf16),
            pltpu.VMEM((4, 2, 64, 256), f32),
            pltpu.VMEM((3, 2, 64, 256), f32),
            pltpu.VMEM((2, 4, 8, 2, 64, 256), bf16),
            pltpu.VMEM((3, 4, 8, 64, 128), bf16),
            pltpu.VMEM((3, 4, 8, 64, 128), bf16),
        ]
        + [pltpu.SemaphoreType.DMA(n) for n in sems],
        compiler_params=pltpu.CompilerParams(
            collective_id=0, has_side_effects=True, vmem_limit_bytes=50 * 1024 * 1024
        ),
        cost_estimate=pl.CostEstimate(flops=4 * 10**9, bytes_accessed=10**7, transcendentals=0),
    )(acts, basis, inverse, projection.T, factor, store.reshape(4, 2, 2, 128, 256))
    return scores.reshape(2048, 128)


def solution(mesh):
    placed = (
        P("store", None),
        P("store", "eig"),
        P(None, "eig"),
        P("eig", None),
        P("store", "eig"),
        P("store", "eig"),
    )
    return jax.shard_map(
        body, mesh=mesh, in_specs=placed, out_specs=P(None, ("store", "eig")), check_vma=False
    )
```

```python
import jax
import jax.numpy as jnp
from jax import lax
from jax.experimental import pallas as pl
from jax.experimental.pallas import tpu as pltpu
from jax.sharding import PartitionSpec as P

damping = 0.1
NT = (((1,), (1,)), ((), ()))


def at(x, zh, c, zl, y):
    return {"eig": x * 4 + zh * 2 + c, "store": zl * 4 + y}


LEVELS = ((0,), (1, 2), (3, 4), (5, 6), (7,))
OFFSETS = (0, 1, 7, 2, 6, 3, 5, 4)


def kernel(
    acts, basis, eigvals, projection, factor, store, out,
    acts_g, basis_g, part, landed, rotated, inv_own, inv_g, proj_g, wide, fac_g, store_g,
    summed, summed_in, feats, going, coming,
    own_sem, basis_sem, az_sem, ax_sem, ac_sem, st_sem, iv_sem, pr_sem, of_sem,
    zr_sem, rc_sem, cx_sem, fz_sem, fy_sem, fc_sem, sx_sem,
):
    e, s = lax.axis_index("eig"), lax.axis_index("store")
    x, zh, c = lax.div(e, 4), lax.rem(lax.div(e, 2), 2), lax.rem(e, 2)
    zl, y = lax.div(s, 4), lax.rem(s, 4)
    z = zh * 4 + zl
    f32, bf16 = jnp.float32, jnp.bfloat16
    sent = []

    def send(src, dst, sems, index, device):
        copy = pltpu.make_async_remote_copy(
            src_ref=src,
            dst_ref=dst,
            send_sem=sems.at[(0, *index)],
            recv_sem=sems.at[(1, *index)],
            device_id=device,
            device_id_type=pl.DeviceIdType.MESH,
        )
        copy.start()
        sent.append(copy)
        return copy

    def off(value, step, extent):
        return lax.rem(value + step, extent)

    def along_x(d):
        return at(off(x, d, 4), zh, c, zl, y)

    def along_y(d):
        return at(x, zh, c, zl, off(y, d, 4))

    def along_z(d):
        to = off(z, d, 8)
        return at(x, lax.div(to, 4), c, lax.rem(to, 4), y)

    def flipped(m, mirror=False):
        to_h = 1 - zh if m & 2 else zh
        to_c = 1 - c if m & 1 else c
        return at(x, to_h, to_c, 3 - zl if mirror and m & 2 else zl, y)

    sibling = flipped(1)

    def block(index, size):
        return pl.ds(pl.multiple_of(index * size, size), size)

    own = [
        pltpu.make_async_copy(basis, basis_g.at[block(y, 512)], own_sem.at[0]),
        pltpu.make_async_copy(acts.at[:, block(zl, 2048)], acts_g.at[0], own_sem.at[1]),
        pltpu.make_async_copy(projection, proj_g.at[0], own_sem.at[2]),
        pltpu.make_async_copy(factor, fac_g.at[0], own_sem.at[3]),
    ]
    for d in range(4):
        own.append(
            pltpu.make_async_copy(
                store.at[off(x, d, 4), zh, c],
                store_g.at[pl.ds(d * 128, 128), block(zh, 256)],
                own_sem.at[4 + d],
            )
        )

    barrier = pltpu.get_barrier_semaphore()
    partners = [along_x(d) for d in range(1, 4)] + [along_y(d) for d in range(1, 4)]
    partners += [along_z(d) for d in range(1, 8)] + [sibling, flipped(3), flipped(3, True)]
    for partner in partners:
        pl.semaphore_signal(barrier, inc=1, device_id=partner, device_id_type=pl.DeviceIdType.MESH)
    for copy in own:
        copy.start()
    for j in range(4):
        rows = 1.0 / (eigvals[j * 16 : j * 16 + 16] + damping)
        for to_c in range(2):
            inv_own[to_c, j] = jnp.concatenate(
                [rows[4 * to_c : 4 * to_c + 4], rows[8 + 4 * to_c : 12 + 4 * to_c]], axis=0
            )
    pl.semaphore_wait(barrier, len(partners))

    mine = block(x * 2 + c, 16)
    line, rings = [], {}
    for h in range(2):
        for d in range(1, 4):
            to = off(zl, d, 4)
            line.append(
                send(
                    acts.at[mine, pl.ds(pl.multiple_of(to * 2048 + h * 1024, 1024), 1024)],
                    acts_g.at[4 - d, mine, pl.ds(h * 1024, 1024)],
                    az_sem, (h, d - 1), at(x, zh, c, to, y),
                )
            )
        if h == 0:
            for n, (half, d) in enumerate(((0, 1), (1, 3), (1, 1), (0, 3))):
                slot = pl.ds(pl.multiple_of(y * 512 + half * 256, 256), 256)
                rings[n] = send(basis.at[pl.ds(half * 256, 256)], basis_g.at[slot], basis_sem, (n,), along_y(d))

    behind = []
    for m in range(1, 4):
        to_c = 1 - c if m & 1 else c
        behind.append(send(inv_own.at[to_c], inv_g.at[m - 1], iv_sem, (m - 1,), flipped(m, True)))
        if m < 3:
            behind.append(send(projection, proj_g.at[m], pr_sem, (m - 1,), flipped(m, True)))
    crossing = behind[3]
    behind.append(send(factor, fac_g.at[1], of_sem, (0,), flipped(2)))

    def offer(m):
        to_h = 1 - zh if m & 2 else zh
        to_c = 1 - c if m & 1 else c
        return [
            send(
                store.at[off(x, d, 4), to_h, to_c],
                store_g.at[pl.ds(d * 128, 128), pl.ds(pl.multiple_of((m & 1) * 512 + zh * 256, 256), 256)],
                st_sem, (m - 1, d), flipped(m),
            )
            for d in range(4)
        ]

    shared, paired = [], []
    for h in range(2):
        for copy in line[3 * h : 3 * h + 3]:
            copy.wait_recv()
        slot = acts_g.at[pl.ds(1, 3), mine, pl.ds(h * 1024, 1024)]
        for dx in (1, 3, 2):
            shared.append((h, dx, send(slot, slot, ax_sem, (h, dx - 1), along_x(dx))))
        paired.append(send(slot, slot, ac_sem, (h, 0), sibling))
    later = offer(2) + offer(1)
    rings[0].wait_recv()
    slot = basis_g.at[pl.ds(pl.multiple_of(off(y, 3, 4) * 512, 256), 256)]
    rings[4] = send(slot, slot, basis_sem, (4,), along_y(1))
    rings[1].wait_recv()
    slot = basis_g.at[pl.ds(pl.multiple_of(off(y, 1, 4) * 512 + 256, 256), 256)]
    rings[5] = send(slot, slot, basis_sem, (5,), along_y(3))
    for h, dx, copy in shared:
        copy.wait_recv()
        slot = acts_g.at[pl.ds(1, 3), block(off(x, 4 - dx, 4) * 2 + c, 16), pl.ds(h * 1024, 1024)]
        paired.append(send(slot, slot, ac_sem, (h, dx), sibling))
    for copy in own[:2]:
        copy.wait()
    for n in range(2, 6):
        rings[n].wait_recv()

    partial = []
    for d in (0, 2, 1, 3):
        if d == 2:
            for copy in paired:
                copy.wait_recv()
        value = jnp.dot(acts_g[d], basis_g[...], preferred_element_type=f32)
        part[d] = value.reshape(2, 64, 512)
        for h in (1, 0):
            if h or d:
                to_h = 1 - zh if h else zh
                partial.append(
                    send(part.at[d, to_h], landed.at[h, d], zr_sem, (h, d), at(x, to_h, c, off(zl, d, 4), y))
                )
    landed[0, 0] = part[0, zh]

    for copy in own[2:]:
        copy.wait()
    crossing.wait_recv()
    behind[2 - 1].wait_recv()
    through = send(proj_g.at[2], proj_g.at[3], pr_sem, (2,), sibling)
    for n, copy in enumerate(behind):
        if n not in (1, 3):
            copy.wait_recv()
    through.wait_recv()
    for m in range(4):
        for k in range(4):
            wide[k * 64 : k * 64 + 64, m * 512 : m * 512 + 512] = proj_g[m]
    spread = (
        lax.div(lax.broadcasted_iota(jnp.int32, (4, 256), 1), 64) == lax.broadcasted_iota(jnp.int32, (4, 256), 0)
    ).astype(f32)
    factors = []
    for h in range(2):
        values = lax.dot_general(
            fac_g[h], spread, (((0,), (0,)), ((), ())),
            preferred_element_type=f32, precision=lax.Precision.HIGHEST,
        )
        factors.append(jnp.where(zh == 0, values[:64], values[64:]))

    for copy in partial:
        copy.wait_recv()
    for h in range(2):
        rotated[0, h] = (landed[h, 0] + landed[h, 1]) + (landed[h, 2] + landed[h, 3])
    across = send(rotated.at[0], rotated.at[1], rc_sem, (0,), sibling)
    later += offer(3)
    across.wait_recv()

    lanes = lax.broadcasted_iota(jnp.int32, (64, 256), 1)
    scattered = []
    for d in (2, 1, 3, 0):
        for h in range(2):
            lefts = []
            for m in range(4):
                source = inv_own.at[c] if m == 0 else inv_g.at[m - 1]
                heights = source[off(x, d, 4)][h * 4 : h * 4 + 4]
                scaled = (rotated[m & 1, m >> 1][None, :, :] * heights[:, None, :]).astype(bf16)
                lefts.append(scaled.reshape(256, 512))
            value = lax.dot_general(
                jnp.concatenate(lefts, axis=1), wide[...], NT, preferred_element_type=f32
            ).reshape(4, 64, 256)
            summed[d, h] = jnp.where(
                lanes < 128,
                jnp.where(lanes < 64, value[0], value[1]),
                jnp.where(lanes < 192, value[2], value[3]),
            )
        if d:
            scattered.append(send(summed.at[d], summed_in.at[d - 1], cx_sem, (d - 1,), along_x(d)))
    for copy in scattered:
        copy.wait_recv()
    for h in range(2):
        total = (summed[0, h] + summed_in[0, h]) + (summed_in[1, h] + summed_in[2, h])
        scale = jnp.where(zh == h, factors[0], factors[1])
        feats[0, 0, :, h * 256 : h * 256 + 256] = (total * scale).astype(bf16)

    def lane(first, count):
        return pl.ds(first * 256, count * 256)

    def slots(level):
        return pl.ds(LEVELS[level][0], len(LEVELS[level]))

    levels, planes, pairs, reduced = {}, {}, {}, {}

    def pair(dy, level):
        pairs[dy, level] = send(
            feats.at[dy, slots(level), :, lane(0, 2)], feats.at[dy, slots(level), :, lane(2, 2)],
            fc_sem, (dy, level), sibling,
        )

    def climb(level):
        if level < 3:
            down = 0 if level == 0 else LEVELS[level][0]
            up = 0 if level == 0 else LEVELS[level][1]
            levels[level + 1] = [
                send(feats.at[0, down, :, lane(0, 2)], feats.at[0, 2 * level + 1, :, lane(0, 2)], fz_sem, (level, 0), along_z(7)),
                send(feats.at[0, up, :, lane(0, 2)], feats.at[0, 2 * level + 2, :, lane(0, 2)], fz_sem, (level, 1), along_z(1)),
            ]
        elif level == 3:
            levels[4] = [
                send(feats.at[0, 5, :, lane(0, 1)], feats.at[0, 7, :, lane(0, 1)], fz_sem, (3, 0), along_z(7)),
                send(feats.at[0, 6, :, lane(1, 1)], feats.at[0, 7, :, lane(1, 1)], fz_sem, (3, 1), along_z(1)),
            ]

    def spread_out(level):
        if level:
            for copy in levels[level]:
                copy.wait_recv()
        climb(level)
        src = feats.at[0, slots(level), :, lane(0, 2)]
        planes[1, level] = send(src, feats.at[3, slots(level), :, lane(0, 2)], fy_sem, (0, level), along_y(1))
        planes[3, level] = send(src, feats.at[1, slots(level), :, lane(0, 2)], fy_sem, (1, level), along_y(3))
        pair(0, level)

    def relay(level):
        planes[1, level].wait_recv()
        planes[2, level] = send(
            feats.at[3, slots(level), :, lane(0, 1)], feats.at[2, slots(level), :, lane(0, 1)],
            fy_sem, (2, level), along_y(1),
        )
        pair(3, level)
        planes[3, level].wait_recv()
        planes[4, level] = send(
            feats.at[1, slots(level), :, lane(1, 1)], feats.at[2, slots(level), :, lane(1, 1)],
            fy_sem, (3, level), along_y(3),
        )
        pair(1, level)

    def relayed(level):
        planes[2, level].wait_recv()
        planes[4, level].wait_recv()
        pair(2, level)

    def place(dy, slot):
        to = off(z, OFFSETS[slot], 8)
        return lax.rem(to, 4), off(y, dy, 4), lax.div(to, 4)

    def score(dy, level):
        pairs[dy, level].wait_recv()
        first, count = LEVELS[level][0], len(LEVELS[level])
        value = lax.dot_general(
            feats[dy, first : first + count].reshape(count * 64, 1024), store_g[...], NT,
            preferred_element_type=f32,
        )
        for n in range(count):
            rows = value[n * 64 : n * 64 + 64]
            for k in range(1, 4):
                going[k - 1, dy, first + n] = rows[:, k * 128 : k * 128 + 128].astype(bf16)
            out[place(dy, first + n)] = rows[:, :128]
        reduced[dy, level] = [
            send(
                going.at[k - 1, dy, slots(level)], coming.at[k - 1, dy, slots(level)],
                sx_sem, (k - 1, dy, level), along_x(k),
            )
            for k in (2, 1, 3)
        ]

    def finish(dy, level):
        for copy in reduced[dy, level]:
            copy.wait_recv()
        for slot in LEVELS[level]:
            rest = coming[0, dy, slot].astype(f32) + coming[1, dy, slot].astype(f32)
            spot = place(dy, slot)
            out[spot] = out[spot] + (rest + coming[2, dy, slot].astype(f32))

    spread_out(0)
    spread_out(1)
    for copy in later:
        copy.wait_recv()
    done = []
    for level in range(5):
        score(0, level)
        if level + 2 < 5:
            spread_out(level + 2)
        relay(level)
        score(3, level)
        score(1, level)
        relayed(level)
        score(2, level)
        if level:
            for dy in (0, 3, 1, 2):
                finish(dy, level - 1)
    for dy in (0, 3, 1, 2):
        finish(dy, 4)
    for copy in sent:
        copy.wait_send()


def body(acts, basis, eigvals, projection, out_factor, store):
    bf16, f32 = jnp.bfloat16, jnp.float32
    sems = [(8,)] + [
        (2, *n)
        for n in [
            (6,), (2, 3), (2, 3), (2, 4), (3, 4), (3,), (3,), (1,), (2, 4), (1,), (3,),
            (4, 2), (4, 5), (4, 5), (3, 4, 5),
        ]
    ]
    vmem = pl.BlockSpec(memory_space=pltpu.VMEM)
    hbm = pl.BlockSpec(memory_space=pl.ANY)
    scores = pl.pallas_call(
        kernel,
        out_shape=jax.ShapeDtypeStruct((4, 4, 2, 64, 128), f32),
        in_specs=[hbm, hbm, vmem, hbm, hbm, hbm],
        out_specs=vmem,
        scratch_shapes=[
            pltpu.VMEM((4, 128, 2048), bf16),
            pltpu.VMEM((2048, 512), bf16),
            pltpu.VMEM((4, 2, 64, 512), f32),
            pltpu.VMEM((2, 4, 64, 512), f32),
            pltpu.VMEM((2, 2, 64, 512), f32),
            pltpu.VMEM((2, 4, 8, 512), f32),
            pltpu.VMEM((3, 4, 8, 512), f32),
            pltpu.VMEM((4, 64, 512), bf16),
            pltpu.VMEM((256, 2048), bf16),
            pltpu.VMEM((2, 4, 128), f32),
            pltpu.VMEM((512, 1024), bf16),
            pltpu.VMEM((4, 2, 64, 256), f32),
            pltpu.VMEM((3, 2, 64, 256), f32),
            pltpu.VMEM((4, 8, 64, 1024), bf16),
            pltpu.VMEM((3, 4, 8, 64, 128), bf16),
            pltpu.VMEM((3, 4, 8, 64, 128), bf16),
        ]
        + [pltpu.SemaphoreType.DMA(n) for n in sems],
        compiler_params=pltpu.CompilerParams(
            collective_id=0, has_side_effects=True, vmem_limit_bytes=60 * 1024 * 1024
        ),
        cost_estimate=pl.CostEstimate(flops=4 * 10**9, bytes_accessed=10**7, transcendentals=0),
    )(acts, basis, eigvals, projection.T, out_factor.T, store.reshape(4, 2, 2, 128, 256))
    return scores.reshape(2048, 128)


def solution(mesh):
    placed = (
        P("store", None),
        P("store", "eig"),
        P(None, "eig"),
        P("eig", None),
        P("store", "eig"),
        P("store", "eig"),
    )
    return jax.shard_map(
        body, mesh=mesh, in_specs=placed, out_specs=P(None, ("store", "eig")), check_vma=False
    )
```

```python
import jax
import jax.numpy as jnp
from jax import lax
from jax.experimental import pallas as pl
from jax.experimental.pallas import tpu as pltpu
from jax.sharding import PartitionSpec as P

damping = 0.1
NT = (((1,), (1,)), ((), ()))


def at(x, zh, c, zl, y):
    return {"eig": x * 4 + zh * 2 + c, "store": zl * 4 + y}


LEVELS = ((0,), (1, 2), (3, 4), (5, 6), (7,))
OFFSETS = (0, 1, 7, 2, 6, 3, 5, 4)


def kernel(
    acts, basis, eigvals, projection, factor, store, out,
    acts_g, basis_g, part, landed, rotated, inv_own, inv_g, proj_g, wide, fac_g, store_g,
    summed, summed_in, feats, going, coming,
    own_sem, basis_sem, az_sem, ax_sem, ac_sem, st_sem, iv_sem, pr_sem, of_sem,
    zr_sem, rc_sem, cx_sem, fz_sem, fy_sem, fc_sem, sx_sem,
):
    e, s = lax.axis_index("eig"), lax.axis_index("store")
    x, zh, c = lax.div(e, 4), lax.rem(lax.div(e, 2), 2), lax.rem(e, 2)
    zl, y = lax.div(s, 4), lax.rem(s, 4)
    z = zh * 4 + zl
    f32, bf16 = jnp.float32, jnp.bfloat16
    sent = []

    def send(src, dst, sems, index, device):
        copy = pltpu.make_async_remote_copy(
            src_ref=src,
            dst_ref=dst,
            send_sem=sems.at[(0, *index)],
            recv_sem=sems.at[(1, *index)],
            device_id=device,
            device_id_type=pl.DeviceIdType.MESH,
        )
        copy.start()
        sent.append(copy)
        return copy

    def off(value, step, extent):
        return lax.rem(value + step, extent)

    def along_x(d):
        return at(off(x, d, 4), zh, c, zl, y)

    def along_y(d):
        return at(x, zh, c, zl, off(y, d, 4))

    def along_z(d):
        to = off(z, d, 8)
        return at(x, lax.div(to, 4), c, lax.rem(to, 4), y)

    def flipped(m, mirror=False):
        to_h = 1 - zh if m & 2 else zh
        to_c = 1 - c if m & 1 else c
        return at(x, to_h, to_c, 3 - zl if mirror and m & 2 else zl, y)

    sibling = flipped(1)

    def block(index, size):
        return pl.ds(pl.multiple_of(index * size, size), size)

    own = [
        pltpu.make_async_copy(basis, basis_g.at[block(y, 512)], own_sem.at[0]),
        pltpu.make_async_copy(acts.at[:, block(zl, 2048)], acts_g.at[0], own_sem.at[1]),
        pltpu.make_async_copy(projection, proj_g.at[0], own_sem.at[2]),
        pltpu.make_async_copy(factor, fac_g.at[0], own_sem.at[3]),
    ]
    for d in range(4):
        own.append(
            pltpu.make_async_copy(
                store.at[off(x, d, 4), zh, c],
                store_g.at[pl.ds(d * 128, 128), block(zh, 256)],
                own_sem.at[4 + d],
            )
        )

    barrier = pltpu.get_barrier_semaphore()
    partners = [along_x(d) for d in range(1, 4)] + [along_y(d) for d in range(1, 4)]
    partners += [along_z(d) for d in range(1, 8)] + [sibling, flipped(3), flipped(3, True)]
    for partner in partners:
        pl.semaphore_signal(barrier, inc=1, device_id=partner, device_id_type=pl.DeviceIdType.MESH)
    for copy in own:
        copy.start()
    for j in range(4):
        rows = 1.0 / (eigvals[j * 16 : j * 16 + 16] + damping)
        for to_c in range(2):
            inv_own[to_c, j] = jnp.concatenate(
                [rows[4 * to_c : 4 * to_c + 4], rows[8 + 4 * to_c : 12 + 4 * to_c]], axis=0
            )
    pl.semaphore_wait(barrier, len(partners))

    mine = block(x * 2 + c, 16)
    line, rings = [], {}
    for h in range(2):
        for d in range(1, 4):
            to = off(zl, d, 4)
            line.append(
                send(
                    acts.at[mine, pl.ds(pl.multiple_of(to * 2048 + h * 1024, 1024), 1024)],
                    acts_g.at[4 - d, mine, pl.ds(h * 1024, 1024)],
                    az_sem, (h, d - 1), at(x, zh, c, to, y),
                )
            )
        if h == 0:
            for n, (half, d) in enumerate(((0, 1), (1, 3), (1, 1), (0, 3))):
                slot = pl.ds(pl.multiple_of(y * 512 + half * 256, 256), 256)
                rings[n] = send(basis.at[pl.ds(half * 256, 256)], basis_g.at[slot], basis_sem, (n,), along_y(d))

    behind = []
    for m in range(1, 4):
        to_c = 1 - c if m & 1 else c
        behind.append(send(inv_own.at[to_c], inv_g.at[m - 1], iv_sem, (m - 1,), flipped(m, True)))
        if m < 3:
            behind.append(send(projection, proj_g.at[m], pr_sem, (m - 1,), flipped(m, True)))
    crossing = behind[3]
    behind.append(send(factor, fac_g.at[1], of_sem, (0,), flipped(2)))

    def offer(m):
        to_h = 1 - zh if m & 2 else zh
        to_c = 1 - c if m & 1 else c
        return [
            send(
                store.at[off(x, d, 4), to_h, to_c],
                store_g.at[pl.ds(d * 128, 128), pl.ds(pl.multiple_of((m & 1) * 512 + zh * 256, 256), 256)],
                st_sem, (m - 1, d), flipped(m),
            )
            for d in range(4)
        ]

    shared, paired = [], []
    for h in range(2):
        for copy in line[3 * h : 3 * h + 3]:
            copy.wait_recv()
        slot = acts_g.at[pl.ds(1, 3), mine, pl.ds(h * 1024, 1024)]
        for dx in (1, 3, 2):
            shared.append((h, dx, send(slot, slot, ax_sem, (h, dx - 1), along_x(dx))))
        paired.append(send(slot, slot, ac_sem, (h, 0), sibling))
    later = offer(2) + offer(1)
    rings[0].wait_recv()
    slot = basis_g.at[pl.ds(pl.multiple_of(off(y, 3, 4) * 512, 256), 256)]
    rings[4] = send(slot, slot, basis_sem, (4,), along_y(1))
    rings[1].wait_recv()
    slot = basis_g.at[pl.ds(pl.multiple_of(off(y, 1, 4) * 512 + 256, 256), 256)]
    rings[5] = send(slot, slot, basis_sem, (5,), along_y(3))
    for h, dx, copy in shared:
        copy.wait_recv()
        slot = acts_g.at[pl.ds(1, 3), block(off(x, 4 - dx, 4) * 2 + c, 16), pl.ds(h * 1024, 1024)]
        paired.append(send(slot, slot, ac_sem, (h, dx), sibling))
    for copy in own[:2]:
        copy.wait()
    for n in range(2, 6):
        rings[n].wait_recv()

    partial = []
    for d in (0, 2, 1, 3):
        if d == 2:
            for copy in paired:
                copy.wait_recv()
        value = jnp.dot(acts_g[d], basis_g[...], preferred_element_type=f32)
        part[d] = value.reshape(2, 64, 512).astype(bf16)
        if d == 0:
            rotated[0, 0] = jnp.where(zh == 0, value[:64], value[64:])
        for h in (1, 0):
            if h or d:
                to_h = 1 - zh if h else zh
                partial.append(
                    send(part.at[d, to_h], landed.at[h, d], zr_sem, (h, d), at(x, to_h, c, off(zl, d, 4), y))
                )

    for copy in own[2:]:
        copy.wait()
    crossing.wait_recv()
    behind[2 - 1].wait_recv()
    through = send(proj_g.at[2], proj_g.at[3], pr_sem, (2,), sibling)
    for n, copy in enumerate(behind):
        if n not in (1, 3):
            copy.wait_recv()
    through.wait_recv()
    for m in range(4):
        for k in range(4):
            wide[k * 64 : k * 64 + 64, m * 512 : m * 512 + 512] = proj_g[m]
    spread = (
        lax.div(lax.broadcasted_iota(jnp.int32, (4, 256), 1), 64) == lax.broadcasted_iota(jnp.int32, (4, 256), 0)
    ).astype(f32)
    factors = []
    for h in range(2):
        values = lax.dot_general(
            fac_g[h], spread, (((0,), (0,)), ((), ())),
            preferred_element_type=f32, precision=lax.Precision.HIGHEST,
        )
        factors.append(jnp.where(zh == 0, values[:64], values[64:]))

    for copy in partial:
        copy.wait_recv()
    for h in range(2):
        first = landed[1, 0].astype(f32) if h else rotated[0, 0]
        rest = landed[h, 2].astype(f32) + landed[h, 3].astype(f32)
        rotated[0, h] = (first + landed[h, 1].astype(f32)) + rest
    across = send(rotated.at[0], rotated.at[1], rc_sem, (0,), sibling)
    later += offer(3)
    across.wait_recv()

    lanes = lax.broadcasted_iota(jnp.int32, (64, 256), 1)
    scattered = []
    for d in (2, 1, 3, 0):
        for h in range(2):
            lefts = []
            for m in range(4):
                source = inv_own.at[c] if m == 0 else inv_g.at[m - 1]
                heights = source[off(x, d, 4)][h * 4 : h * 4 + 4]
                scaled = (rotated[m & 1, m >> 1][None, :, :] * heights[:, None, :]).astype(bf16)
                lefts.append(scaled.reshape(256, 512))
            value = lax.dot_general(
                jnp.concatenate(lefts, axis=1), wide[...], NT, preferred_element_type=f32
            ).reshape(4, 64, 256)
            summed[d, h] = jnp.where(
                lanes < 128,
                jnp.where(lanes < 64, value[0], value[1]),
                jnp.where(lanes < 192, value[2], value[3]),
            )
        if d:
            scattered.append(send(summed.at[d], summed_in.at[d - 1], cx_sem, (d - 1,), along_x(d)))
    for copy in scattered:
        copy.wait_recv()
    for h in range(2):
        total = (summed[0, h] + summed_in[0, h]) + (summed_in[1, h] + summed_in[2, h])
        scale = jnp.where(zh == h, factors[0], factors[1])
        feats[0, 0, :, h * 256 : h * 256 + 256] = (total * scale).astype(bf16)

    def lane(first, count):
        return pl.ds(first * 256, count * 256)

    def slots(level):
        return pl.ds(LEVELS[level][0], len(LEVELS[level]))

    levels, planes, pairs, reduced = {}, {}, {}, {}

    def pair(dy, level):
        pairs[dy, level] = send(
            feats.at[dy, slots(level), :, lane(0, 2)], feats.at[dy, slots(level), :, lane(2, 2)],
            fc_sem, (dy, level), sibling,
        )

    def climb(level):
        if level < 3:
            down = 0 if level == 0 else LEVELS[level][0]
            up = 0 if level == 0 else LEVELS[level][1]
            levels[level + 1] = [
                send(feats.at[0, down, :, lane(0, 2)], feats.at[0, 2 * level + 1, :, lane(0, 2)], fz_sem, (level, 0), along_z(7)),
                send(feats.at[0, up, :, lane(0, 2)], feats.at[0, 2 * level + 2, :, lane(0, 2)], fz_sem, (level, 1), along_z(1)),
            ]
        elif level == 3:
            levels[4] = [
                send(feats.at[0, 5, :, lane(0, 1)], feats.at[0, 7, :, lane(0, 1)], fz_sem, (3, 0), along_z(7)),
                send(feats.at[0, 6, :, lane(1, 1)], feats.at[0, 7, :, lane(1, 1)], fz_sem, (3, 1), along_z(1)),
            ]

    def spread_out(level):
        if level:
            for copy in levels[level]:
                copy.wait_recv()
        climb(level)
        src = feats.at[0, slots(level), :, lane(0, 2)]
        planes[1, level] = send(src, feats.at[3, slots(level), :, lane(0, 2)], fy_sem, (0, level), along_y(1))
        planes[3, level] = send(src, feats.at[1, slots(level), :, lane(0, 2)], fy_sem, (1, level), along_y(3))
        pair(0, level)

    def relay(level):
        planes[1, level].wait_recv()
        planes[2, level] = send(
            feats.at[3, slots(level), :, lane(0, 1)], feats.at[2, slots(level), :, lane(0, 1)],
            fy_sem, (2, level), along_y(1),
        )
        pair(3, level)
        planes[3, level].wait_recv()
        planes[4, level] = send(
            feats.at[1, slots(level), :, lane(1, 1)], feats.at[2, slots(level), :, lane(1, 1)],
            fy_sem, (3, level), along_y(3),
        )
        pair(1, level)

    def relayed(level):
        planes[2, level].wait_recv()
        planes[4, level].wait_recv()
        pair(2, level)

    def place(dy, slot):
        to = off(z, OFFSETS[slot], 8)
        return lax.rem(to, 4), off(y, dy, 4), lax.div(to, 4)

    def score(dy, level):
        pairs[dy, level].wait_recv()
        first, count = LEVELS[level][0], len(LEVELS[level])
        value = lax.dot_general(
            feats[dy, first : first + count].reshape(count * 64, 1024), store_g[...], NT,
            preferred_element_type=f32,
        )
        for n in range(count):
            rows = value[n * 64 : n * 64 + 64]
            for k in range(1, 4):
                going[k - 1, dy, first + n] = rows[:, k * 128 : k * 128 + 128].astype(bf16)
            out[place(dy, first + n)] = rows[:, :128]
        reduced[dy, level] = [
            send(
                going.at[k - 1, dy, slots(level)], coming.at[k - 1, dy, slots(level)],
                sx_sem, (k - 1, dy, level), along_x(k),
            )
            for k in (2, 1, 3)
        ]

    def finish(dy, level):
        for copy in reduced[dy, level]:
            copy.wait_recv()
        for slot in LEVELS[level]:
            rest = coming[0, dy, slot].astype(f32) + coming[1, dy, slot].astype(f32)
            spot = place(dy, slot)
            out[spot] = out[spot] + (rest + coming[2, dy, slot].astype(f32))

    for step in range(9):
        if step < 5:
            spread_out(step)
            if step == 0:
                for copy in later:
                    copy.wait_recv()
            score(0, step)
        if 0 <= step - 1 < 5:
            relay(step - 1)
            score(3, step - 1)
            score(1, step - 1)
        if 0 <= step - 2 < 5:
            relayed(step - 2)
            score(2, step - 2)
        if step >= 4:
            for dy in (0, 3, 1, 2):
                finish(dy, step - 4)
    for copy in sent:
        copy.wait_send()


def body(acts, basis, eigvals, projection, out_factor, store):
    bf16, f32 = jnp.bfloat16, jnp.float32
    sems = [(8,)] + [
        (2, *n)
        for n in [
            (6,), (2, 3), (2, 3), (2, 4), (3, 4), (3,), (3,), (1,), (2, 4), (1,), (3,),
            (4, 2), (4, 5), (4, 5), (3, 4, 5),
        ]
    ]
    vmem = pl.BlockSpec(memory_space=pltpu.VMEM)
    hbm = pl.BlockSpec(memory_space=pl.ANY)
    scores = pl.pallas_call(
        kernel,
        out_shape=jax.ShapeDtypeStruct((4, 4, 2, 64, 128), f32),
        in_specs=[hbm, hbm, vmem, hbm, hbm, hbm],
        out_specs=vmem,
        scratch_shapes=[
            pltpu.VMEM((4, 128, 2048), bf16),
            pltpu.VMEM((2048, 512), bf16),
            pltpu.VMEM((4, 2, 64, 512), bf16),
            pltpu.VMEM((2, 4, 64, 512), bf16),
            pltpu.VMEM((2, 2, 64, 512), f32),
            pltpu.VMEM((2, 4, 8, 512), f32),
            pltpu.VMEM((3, 4, 8, 512), f32),
            pltpu.VMEM((4, 64, 512), bf16),
            pltpu.VMEM((256, 2048), bf16),
            pltpu.VMEM((2, 4, 128), f32),
            pltpu.VMEM((512, 1024), bf16),
            pltpu.VMEM((4, 2, 64, 256), f32),
            pltpu.VMEM((3, 2, 64, 256), f32),
            pltpu.VMEM((4, 8, 64, 1024), bf16),
            pltpu.VMEM((3, 4, 8, 64, 128), bf16),
            pltpu.VMEM((3, 4, 8, 64, 128), bf16),
        ]
        + [pltpu.SemaphoreType.DMA(n) for n in sems],
        compiler_params=pltpu.CompilerParams(
            collective_id=0, has_side_effects=True, vmem_limit_bytes=60 * 1024 * 1024
        ),
        cost_estimate=pl.CostEstimate(flops=4 * 10**9, bytes_accessed=10**7, transcendentals=0),
    )(acts, basis, eigvals, projection.T, out_factor.T, store.reshape(4, 2, 2, 128, 256))
    return scores.reshape(2048, 128)


def solution(mesh):
    placed = (
        P("store", None),
        P("store", "eig"),
        P(None, "eig"),
        P("eig", None),
        P("store", "eig"),
        P("store", "eig"),
    )
    return jax.shard_map(
        body, mesh=mesh, in_specs=placed, out_specs=P(None, ("store", "eig")), check_vma=False
    )
```

```python
import jax
import jax.numpy as jnp
from jax import lax
from jax.experimental import pallas as pl
from jax.experimental.pallas import tpu as pltpu
from jax.sharding import PartitionSpec as P

damping = 0.1
NT = (((1,), (1,)), ((), ()))
NN = (((1,), (0,)), ((), ()))


def at(x, zh, c, zl, y):
    return {"eig": x * 4 + zh * 2 + c, "store": zl * 4 + y}


DIRECT = (0, 4)
LEVELS = ((0,), (1, 2), (3, 4), (5, 6), (7,))
OFFSETS = (0, 1, 7, 2, 6, 3, 5, 4)


def kernel(
    acts, basis, eigvals, projection, factor, store, out,
    acts_g, basis_g, part, landed, rotated, inv_own, inv_g, proj_g, wide, fac_g, store_g, store_t,
    halfway, summed, summed_in, feats, going, coming,
    own_sem, basis_sem, az_sem, ax_sem, ac_sem, st_sem, iv_sem, pr_sem, of_sem,
    zr_sem, rc_sem, cx_sem, fz_sem, fy_sem, fc_sem, sx_sem,
):
    e, s = lax.axis_index("eig"), lax.axis_index("store")
    x, zh, c = lax.div(e, 4), lax.rem(lax.div(e, 2), 2), lax.rem(e, 2)
    zl, y = lax.div(s, 4), lax.rem(s, 4)
    z = zh * 4 + zl
    f32, bf16 = jnp.float32, jnp.bfloat16
    sent = []

    def send(src, dst, sems, index, device):
        copy = pltpu.make_async_remote_copy(
            src_ref=src,
            dst_ref=dst,
            send_sem=sems.at[(0, *index)],
            recv_sem=sems.at[(1, *index)],
            device_id=device,
            device_id_type=pl.DeviceIdType.MESH,
        )
        copy.start()
        sent.append(copy)
        return copy

    def off(value, step, extent):
        return lax.rem(value + step, extent)

    def along_x(d):
        return at(off(x, d, 4), zh, c, zl, y)

    def along_y(d):
        return at(x, zh, c, zl, off(y, d, 4))

    def along_z(d):
        to = off(z, d, 8)
        return at(x, lax.div(to, 4), c, lax.rem(to, 4), y)

    def flipped(m, mirror=False):
        to_h = 1 - zh if m & 2 else zh
        to_c = 1 - c if m & 1 else c
        return at(x, to_h, to_c, 3 - zl if mirror and m & 2 else zl, y)

    sibling = flipped(1)

    def block(index, size):
        return pl.ds(pl.multiple_of(index * size, size), size)

    own = [
        pltpu.make_async_copy(basis, basis_g.at[block(y, 512)], own_sem.at[0]),
        pltpu.make_async_copy(acts.at[:, block(zl, 2048)], acts_g.at[0], own_sem.at[1]),
        pltpu.make_async_copy(projection, proj_g.at[0], own_sem.at[2]),
        pltpu.make_async_copy(factor, fac_g.at[0], own_sem.at[3]),
    ]
    for d in range(4):
        own.append(
            pltpu.make_async_copy(
                store.at[off(x, d, 4), zh, c],
                store_g.at[pl.ds(d * 128, 128), block(zh, 256)],
                own_sem.at[4 + d],
            )
        )

    barrier = pltpu.get_barrier_semaphore()
    partners = [along_x(d) for d in range(1, 4)] + [along_y(d) for d in range(1, 4)]
    partners += [along_z(d) for d in range(1, 8)] + [sibling, flipped(3), flipped(3, True)]
    for partner in partners:
        pl.semaphore_signal(barrier, inc=1, device_id=partner, device_id_type=pl.DeviceIdType.MESH)
    for copy in own:
        copy.start()
    for j in range(4):
        rows = 1.0 / (eigvals[j * 16 : j * 16 + 16] + damping)
        for to_c in range(2):
            inv_own[to_c, j] = jnp.concatenate(
                [rows[4 * to_c : 4 * to_c + 4], rows[8 + 4 * to_c : 12 + 4 * to_c]], axis=0
            )
    pl.semaphore_wait(barrier, len(partners))

    mine = block(x * 2 + c, 16)
    line, rings = {}, {}
    for d in (1, 3, 2):
        to = off(zl, d, 4)
        line[d] = send(
            acts.at[mine, block(to, 2048)], acts_g.at[4 - d, mine], az_sem, (d - 1,), at(x, zh, c, to, y)
        )

    def quarter(at_y, half, j):
        rows = pl.ds(pl.multiple_of(at_y * 512 + half * 256, 256), 256)
        return basis_g.at[rows, pl.ds(j * 256, 256)]

    for j in range(2):
        for n, (half, d) in enumerate(((0, 1), (1, 3), (1, 1), (0, 3))):
            rings[j, n] = send(
                basis.at[pl.ds(half * 256, 256), pl.ds(j * 256, 256)], quarter(y, half, j),
                basis_sem, (j, n), along_y(d),
            )

    behind = []
    for m in range(1, 4):
        to_c = 1 - c if m & 1 else c
        behind.append(send(inv_own.at[to_c], inv_g.at[m - 1], iv_sem, (m - 1,), flipped(m, True)))
        if m < 3:
            behind.append(send(projection, proj_g.at[m], pr_sem, (m - 1,), flipped(m, True)))
    crossing = behind[3]
    behind.append(send(factor, fac_g.at[1], of_sem, (0,), flipped(2)))

    def offer(m):
        to_h = 1 - zh if m & 2 else zh
        to_c = 1 - c if m & 1 else c
        return [
            send(
                store.at[off(x, d, 4), to_h, to_c],
                store_g.at[pl.ds(d * 128, 128), pl.ds(pl.multiple_of((m & 1) * 512 + zh * 256, 256), 256)],
                st_sem, (m - 1, d), flipped(m),
            )
            for d in range(4)
        ]

    shared, paired, partial = {}, {1: [], 2: [], 3: []}, []
    for d in (1, 3, 2):
        line[d].wait_recv()
        slot = acts_g.at[4 - d, mine]
        shared[d] = [(dx, send(slot, slot, ax_sem, (d - 1, dx - 1), along_x(dx))) for dx in (1, 3, 2)]
        paired[d].append(send(slot, slot, ac_sem, (d - 1, 0), sibling))
    later = offer(2) + offer(1)

    def pass_on(j):
        rings[j, 0].wait_recv()
        slot = quarter(off(y, 3, 4), 0, j)
        rings[j, 4] = send(slot, slot, basis_sem, (j, 4), along_y(1))
        rings[j, 1].wait_recv()
        slot = quarter(off(y, 1, 4), 1, j)
        rings[j, 5] = send(slot, slot, basis_sem, (j, 5), along_y(3))

    def share(d):
        for dx, copy in shared[d]:
            copy.wait_recv()
            slot = acts_g.at[4 - d, block(off(x, 4 - dx, 4) * 2 + c, 16)]
            paired[d].append(send(slot, slot, ac_sem, (d - 1, dx), sibling))

    def rotate(d, j):
        cols = slice(j * 256, j * 256 + 256)
        value = jnp.dot(acts_g[d], basis_g[:, cols], preferred_element_type=f32)
        part[d, :, :, cols] = value.reshape(2, 64, 256).astype(bf16)
        if d == 0:
            rotated[0, 0, :, cols] = jnp.where(zh == 0, value[:64], value[64:])
        for h in (1, 0):
            if h or d:
                to_h = 1 - zh if h else zh
                piece = pl.ds(j * 256, 256)
                partial.append(
                    send(
                        part.at[d, to_h, :, piece], landed.at[h, d, :, piece],
                        zr_sem, (j, h, d), at(x, to_h, c, off(zl, d, 4), y),
                    )
                )

    pass_on(0)
    share(1)
    for copy in own[:2]:
        copy.wait()
    for n in range(2, 6):
        rings[0, n].wait_recv()
    rotate(0, 0)
    pass_on(1)
    for d in (1, 3, 2):
        if d != 2:
            share(4 - d if d == 1 else 2)
        for copy in paired[d]:
            copy.wait_recv()
        rotate(4 - d, 0)
    for n in range(2, 6):
        rings[1, n].wait_recv()
    for d in (2, 1, 3, 0):
        rotate(d, 1)

    for copy in own[2:]:
        copy.wait()
    crossing.wait_recv()
    behind[2 - 1].wait_recv()
    through = send(proj_g.at[2], proj_g.at[3], pr_sem, (2,), sibling)
    for n, copy in enumerate(behind):
        if n not in (1, 3):
            copy.wait_recv()
    through.wait_recv()
    for n, m in enumerate((0, 2, 1, 3)):
        for k in range(4):
            wide[k * 64 : k * 64 + 64, n * 512 : n * 512 + 512] = proj_g[m]
    spread = (
        lax.div(lax.broadcasted_iota(jnp.int32, (4, 256), 1), 64) == lax.broadcasted_iota(jnp.int32, (4, 256), 0)
    ).astype(f32)
    factors = []
    for h in range(2):
        values = lax.dot_general(
            fac_g[h], spread, (((0,), (0,)), ((), ())),
            preferred_element_type=f32, precision=lax.Precision.HIGHEST,
        )
        factors.append(jnp.where(zh == 0, values[:64], values[64:]))

    def turn_over(m):
        at_h = 1 - zh if m & 2 else zh
        place_of = pl.ds(pl.multiple_of((m & 1) * 512 + at_h * 256, 256), 256)
        store_t[place_of] = store_g[:, place_of].T

    for copy in later:
        copy.wait_recv()
    for m in range(3):
        turn_over(m)

    for copy in partial:
        copy.wait_recv()
    for h in range(2):
        first = landed[1, 0].astype(f32) if h else rotated[0, 0]
        rest = landed[h, 2].astype(f32) + landed[h, 3].astype(f32)
        rotated[0, h] = (first + landed[h, 1].astype(f32)) + rest
    across = send(rotated.at[0], rotated.at[1], rc_sem, (0,), sibling)
    last = offer(3)

    def project(d, h, core):
        lefts = []
        for m in (core, core + 2):
            source = inv_own.at[c] if m == 0 else inv_g.at[m - 1]
            heights = source[off(x, d, 4)][h * 4 : h * 4 + 4]
            scaled = (rotated[core, m >> 1][None, :, :] * heights[:, None, :]).astype(bf16)
            lefts.append(scaled.reshape(256, 512))
        return lax.dot_general(
            jnp.concatenate(lefts, axis=1), wide[:, core * 1024 : core * 1024 + 1024], NT,
            preferred_element_type=f32,
        )

    for d in (2, 1, 3, 0):
        for h in range(2):
            halfway[d, h] = project(d, h, 0)
    across.wait_recv()
    lanes = lax.broadcasted_iota(jnp.int32, (64, 256), 1)
    scattered = []
    for d in (2, 1, 3, 0):
        for h in range(2):
            value = (halfway[d, h] + project(d, h, 1)).reshape(4, 64, 256)
            summed[d, h] = jnp.where(
                lanes < 128,
                jnp.where(lanes < 64, value[0], value[1]),
                jnp.where(lanes < 192, value[2], value[3]),
            )
        if d:
            scattered.append(send(summed.at[d], summed_in.at[d - 1], cx_sem, (d - 1,), along_x(d)))
    for copy in scattered:
        copy.wait_recv()
    for h in range(2):
        total = (summed[0, h] + summed_in[0, h]) + (summed_in[1, h] + summed_in[2, h])
        scale = jnp.where(zh == h, factors[0], factors[1])
        feats[0, 0, :, h * 256 : h * 256 + 256] = (total * scale).astype(bf16)

    def lane(first, count):
        return pl.ds(first * 256, count * 256)

    def slots(level):
        return pl.ds(LEVELS[level][0], len(LEVELS[level]))

    levels, planes, pairs, reduced = {}, {}, {}, {}

    def pair(dy, level):
        pairs[dy, level] = send(
            feats.at[dy, slots(level), :, lane(0, 2)], feats.at[dy, slots(level), :, lane(2, 2)],
            fc_sem, (dy, level), sibling,
        )

    def climb(level):
        if level < 3:
            down = 0 if level == 0 else LEVELS[level][0]
            up = 0 if level == 0 else LEVELS[level][1]
            levels[level + 1] = [
                send(feats.at[0, down, :, lane(0, 2)], feats.at[0, 2 * level + 1, :, lane(0, 2)], fz_sem, (level, 0), along_z(7)),
                send(feats.at[0, up, :, lane(0, 2)], feats.at[0, 2 * level + 2, :, lane(0, 2)], fz_sem, (level, 1), along_z(1)),
            ]
        elif level == 3:
            levels[4] = [
                send(feats.at[0, 5, :, lane(0, 1)], feats.at[0, 7, :, lane(0, 1)], fz_sem, (3, 0), along_z(7)),
                send(feats.at[0, 6, :, lane(1, 1)], feats.at[0, 7, :, lane(1, 1)], fz_sem, (3, 1), along_z(1)),
            ]

    def spread_out(level):
        if level:
            for copy in levels[level]:
                copy.wait_recv()
        climb(level)
        src = feats.at[0, slots(level), :, lane(0, 2)]
        if level in DIRECT:
            far = feats.at[2, slots(level), :, lane(0, 2)]
            planes[2, level] = send(src, far, fy_sem, (2, level), along_y(2))
        planes[1, level] = send(src, feats.at[3, slots(level), :, lane(0, 2)], fy_sem, (0, level), along_y(1))
        planes[3, level] = send(src, feats.at[1, slots(level), :, lane(0, 2)], fy_sem, (1, level), along_y(3))
        pair(0, level)

    def relay(level):
        planes[1, level].wait_recv()
        if level not in DIRECT:
            planes[2, level] = send(
                feats.at[3, slots(level), :, lane(0, 1)], feats.at[2, slots(level), :, lane(0, 1)],
                fy_sem, (2, level), along_y(1),
            )
        pair(3, level)
        planes[3, level].wait_recv()
        if level not in DIRECT:
            planes[4, level] = send(
                feats.at[1, slots(level), :, lane(1, 1)], feats.at[2, slots(level), :, lane(1, 1)],
                fy_sem, (3, level), along_y(3),
            )
        pair(1, level)

    def relayed(level):
        planes[2, level].wait_recv()
        if level not in DIRECT:
            planes[4, level].wait_recv()
        pair(2, level)

    def place(dy, slot):
        to = off(z, OFFSETS[slot], 8)
        return lax.rem(to, 4), off(y, dy, 4), lax.div(to, 4)

    def score(dy, level):
        pairs[dy, level].wait_recv()
        first, count = LEVELS[level][0], len(LEVELS[level])
        value = lax.dot_general(
            feats[dy, first : first + count].reshape(count * 64, 1024), store_t[...],
            NN, preferred_element_type=f32,
        )
        for n in range(count):
            rows = value[n * 64 : n * 64 + 64]
            for k in range(1, 4):
                going[k - 1, dy, first + n] = rows[:, k * 128 : k * 128 + 128].astype(bf16)
            out[place(dy, first + n)] = rows[:, :128]
        reduced[dy, level] = [
            send(
                going.at[k - 1, dy, slots(level)], coming.at[k - 1, dy, slots(level)],
                sx_sem, (k - 1, dy, level), along_x(k),
            )
            for k in (2, 1, 3)
        ]

    def finish(dy, level):
        for copy in reduced[dy, level]:
            copy.wait_recv()
        for slot in LEVELS[level]:
            rest = coming[0, dy, slot].astype(f32) + coming[1, dy, slot].astype(f32)
            spot = place(dy, slot)
            out[spot] = out[spot] + (rest + coming[2, dy, slot].astype(f32))

    for step in range(9):
        if step < 5:
            spread_out(step)
        if step == 0:
            for copy in last:
                copy.wait_recv()
            turn_over(3)
        if 0 <= step - 1 < 5:
            relay(step - 1)
        if step < 5:
            score(0, step)
        if 0 <= step - 1 < 5:
            score(3, step - 1)
            score(1, step - 1)
        if 0 <= step - 2 < 5:
            relayed(step - 2)
            score(2, step - 2)
        if step >= 4:
            for dy in (0, 3, 1, 2):
                finish(dy, step - 4)
    for copy in sent:
        copy.wait_send()


def body(acts, basis, eigvals, projection, out_factor, store):
    bf16, f32 = jnp.bfloat16, jnp.float32
    sems = [(8,)] + [
        (2, *n)
        for n in [
            (2, 6), (3,), (3, 3), (3, 4), (3, 4), (3,), (3,), (1,), (2, 2, 4), (1,), (3,),
            (4, 2), (4, 5), (4, 5), (3, 4, 5),
        ]
    ]
    vmem = pl.BlockSpec(memory_space=pltpu.VMEM)
    hbm = pl.BlockSpec(memory_space=pl.ANY)
    scores = pl.pallas_call(
        kernel,
        out_shape=jax.ShapeDtypeStruct((4, 4, 2, 64, 128), f32),
        in_specs=[hbm, hbm, vmem, hbm, hbm, hbm],
        out_specs=vmem,
        scratch_shapes=[
            pltpu.VMEM((4, 128, 2048), bf16),
            pltpu.VMEM((2048, 512), bf16),
            pltpu.VMEM((4, 2, 64, 512), bf16),
            pltpu.VMEM((2, 4, 64, 512), bf16),
            pltpu.VMEM((2, 2, 64, 512), f32),
            pltpu.VMEM((2, 4, 8, 512), f32),
            pltpu.VMEM((3, 4, 8, 512), f32),
            pltpu.VMEM((4, 64, 512), bf16),
            pltpu.VMEM((256, 2048), bf16),
            pltpu.VMEM((2, 4, 128), f32),
            pltpu.VMEM((512, 1024), bf16),
            pltpu.VMEM((1024, 512), bf16),
            pltpu.VMEM((4, 2, 256, 256), f32),
            pltpu.VMEM((4, 2, 64, 256), f32),
            pltpu.VMEM((3, 2, 64, 256), f32),
            pltpu.VMEM((4, 8, 64, 1024), bf16),
            pltpu.VMEM((3, 4, 8, 64, 128), bf16),
            pltpu.VMEM((3, 4, 8, 64, 128), bf16),
        ]
        + [pltpu.SemaphoreType.DMA(n) for n in sems],
        compiler_params=pltpu.CompilerParams(
            collective_id=0, has_side_effects=True, vmem_limit_bytes=60 * 1024 * 1024
        ),
        cost_estimate=pl.CostEstimate(flops=4 * 10**9, bytes_accessed=10**7, transcendentals=0),
    )(acts, basis, eigvals, projection.T, out_factor.T, store.reshape(4, 2, 2, 128, 256))
    return scores.reshape(2048, 128)


def solution(mesh):
    placed = (
        P("store", None),
        P("store", "eig"),
        P(None, "eig"),
        P("eig", None),
        P("store", "eig"),
        P("store", "eig"),
    )
    return jax.shard_map(
        body, mesh=mesh, in_specs=placed, out_specs=P(None, ("store", "eig")), check_vma=False
    )
```
